32 devices in a mesh: grp: 4 (over z), seq: 4 (over y, x), mdl: 2 (over core).
Axes of the slice: x: 2, y: 2, z: 4, core: 2. Of those that a mesh axis runs over, the one named last changes fastest.
Arguments:
- tree_states: bfloat16 [16, 64, 16384], P('grp', None, 'seq'), may hold values from -400 to 400
- attn_gain: bfloat16 [16384], P('seq'), may hold values from 0.099609375 to 1.8984375
- w_query: bfloat16 [16384, 8192], P('seq', 'mdl'), may hold values from -0.046875 to 0.046875
- w_key: bfloat16 [16384, 512], P('seq', 'mdl'), may hold values from -0.046875 to 0.046875
- w_value: bfloat16 [16384, 512], P('seq', 'mdl'), may hold values from -0.046875 to 0.046875
- w_out: bfloat16 [8192, 16384], P('mdl', 'seq'), may hold values from -0.0625 to 0.0625
- k_cache: bfloat16 [16, 8192, 512], P('grp', 'seq', 'mdl'), may hold values from -72 to 72
- v_cache: bfloat16 [16, 8192, 512], P('grp', 'seq', 'mdl'), may hold values from -12 to 12
- hist_lens: int32 [16], P('grp'), may hold values from 16 to 8192, as said below
- parents: int32 [16, 64], P('grp'), may hold values from 0 to 62, as said below
- low_feats: bfloat16 [16, 64, 16384], P('grp', None, 'seq'), may hold values from -400 to 400
- mid_feats: bfloat16 [16, 64, 16384], P('grp', None, 'seq'), may hold values from -400 to 400
- join_weight: bfloat16 [3, 16384, 8192], P(None, 'seq', ('grp', 'mdl')), may hold values from -0.1171875 to 0.1171875
- draft_gain: bfloat16 [8192], P(('grp', 'mdl')), may hold values from 0.099609375 to 1.8984375
Outputs:
- attn_branch: bfloat16 [16, 64, 16384], P('grp', None, 'seq')
- draft_input: bfloat16 [16, 64, 8192], P(None, 'seq', ('grp', 'mdl'))
The draws below stay inside these ranges and needn't reach their ends.
Inputs may be any that keep to these rules, and one draw needn't show every extreme that they name: `hist_lens`: every conversation has 16 to 8192 live cache positions; in every draw one conversation has 8192 and another fewer than 32. parents[c, 0] = 0 for the root; for node i >= 1 the parent lies in max(0, i - 4) to i - 1.
All inputs are finite; a program needn't handle non-finite values.
Results may differ from the reference program's by a relative error of at most 0.011.
Values may be sent and summed in bfloat16 or wider, within the bound.
A program may use at most 256 MiB of HBM per device.

```python
import math
import jax
import jax.numpy as jnp
from jax import lax

D = 16384
HEADS = 64
KV_HEADS = 4
HEAD_DIM = 128
DRAFT_OUT = 8192
TREE = 64
HIST = 8192
CONV = 16


def scaled_features(key):
    noise_key, row_key, col_key = jax.random.split(key, 3)
    noise = jnp.clip(jax.random.normal(noise_key, (CONV, TREE, D), jnp.float32), -5.0, 5.0)
    row_scale = jnp.exp(jax.random.uniform(row_key, (CONV, TREE, 1), jnp.float32, 0.0, math.log(10.0)))
    rough = jnp.exp(jax.random.uniform(col_key, (D,), jnp.float32, math.log(0.3), math.log(3.0)))
    ramp = jnp.arange(D, dtype=jnp.float32) / (D - 1)
    column = jnp.sqrt((1.0 + 2.0 * ramp) * rough)
    return noise * row_scale * column


def draw_tree_states(key, part):
    return scaled_features(jax.random.fold_in(key, 101)).astype(jnp.bfloat16)


def draw_low_feats(key, part):
    return scaled_features(jax.random.fold_in(key, 202)).astype(jnp.bfloat16)


def draw_mid_feats(key, part):
    return scaled_features(jax.random.fold_in(key, 303)).astype(jnp.bfloat16)


def draw_k_cache(key, part):
    noise_key = jax.random.fold_in(jax.random.fold_in(key, 404), 0)
    width_all = KV_HEADS * HEAD_DIM
    noise = jnp.clip(jax.random.normal(noise_key, (CONV, HIST, width_all), jnp.float32), -5.0, 5.0)
    return noise.astype(jnp.bfloat16)


def draw_v_cache(key, part):
    noise_key, block_key = jax.random.split(jax.random.fold_in(key, 505), 2)
    width_all = KV_HEADS * HEAD_DIM
    blocks = 64
    noise = jnp.clip(jax.random.normal(noise_key, (CONV, blocks, HIST // blocks, width_all), jnp.float32), -5.0, 5.0)
    offsets = jnp.clip(jax.random.normal(block_key, (CONV, blocks, 1, width_all), jnp.float32), -4.0, 4.0)
    return (noise + offsets).reshape(CONV, HIST, width_all).astype(jnp.bfloat16)


def draw_join_weight(key, part):
    noise_key, col_key = jax.random.split(jax.random.fold_in(key, 606), 2)
    noise = jnp.clip(jax.random.normal(noise_key, (3, D, DRAFT_OUT), jnp.float32), -5.0, 5.0) / math.sqrt(3 * D)
    rough = jnp.exp(jax.random.uniform(col_key, (DRAFT_OUT,), jnp.float32, math.log(0.3), math.log(3.0)))
    ramp = jnp.arange(DRAFT_OUT, dtype=jnp.float32) / (DRAFT_OUT - 1)
    column = jnp.sqrt((1.0 + 2.0 * ramp) * rough)
    return (noise * column).astype(jnp.bfloat16)


def draw_hist_lens(key, part):
    mant_key, expo_key, full_key, short_key = jax.random.split(jax.random.fold_in(key, 707), 4)
    top_shift = (HIST // 32).bit_length() - 1
    mantissa = jax.random.randint(mant_key, (CONV,), 16, 32, dtype=jnp.int32)
    exponent = jax.random.randint(expo_key, (CONV,), 0, top_shift + 1, dtype=jnp.int32)
    lengths = jnp.minimum(jnp.left_shift(mantissa, exponent), HIST)
    full_slot = jax.random.randint(full_key, (), 0, CONV, dtype=jnp.int32)
    short_slot = (full_slot + jax.random.randint(short_key, (), 1, CONV, dtype=jnp.int32)) % CONV
    indices = jnp.arange(CONV, dtype=jnp.int32)
    lengths = jnp.where(indices == full_slot, HIST, lengths)
    lengths = jnp.where(indices == short_slot, mantissa, lengths)
    return lengths.astype(jnp.int32)


def draw_parents(key, part):
    backward = jax.random.randint(jax.random.fold_in(key, 808), (CONV, TREE), 0, 4, dtype=jnp.int32)
    indices = jnp.arange(TREE, dtype=jnp.int32)[None, :]
    return jnp.maximum(indices - 1 - backward, 0).astype(jnp.int32)


def shard_levels(rng, dims, cuts, low, high):
    gain, own = 1.0, jax.random.fold_in(rng, 6)
    for axis_at, parts in cuts:
        heights = jnp.exp(jax.random.uniform(jax.random.fold_in(own, axis_at), (parts,), jnp.float32, low / len(cuts), high / len(cuts)))
        gain = gain * jnp.repeat(heights, dims[axis_at] // parts).reshape([-1 if axis == axis_at else 1 for axis in range(len(dims))])
    return gain


def scatter_about(rng, extent, scale, reach, cuts=(), held_as=jnp.bfloat16):
    array = jax.random.normal(rng, extent, jnp.float32) * scale
    if len(cuts) > 0:
        array = shard_levels(rng, extent, cuts, -0.22, 0.18) * array
    return jnp.clip(array, min=-reach, max=reach).astype(held_as)


def setup_inputs(seed: int = 0) -> dict:
    seeds = jax.random.split(jax.random.key(seed), 15)
    tree_states = draw_tree_states(jax.random.fold_in(seeds[14], 71), 0)
    attn_gain = jnp.clip(1.0 + 0.18 * jax.random.normal(seeds[1], (D,), jnp.float32), 0.099609375, 1.8984375).astype(jnp.bfloat16)
    w_query = scatter_about(seeds[2], (D, HEADS * HEAD_DIM), D ** -0.5, 0.046875, ((0, 4), (1, 2)))
    w_key = scatter_about(seeds[3], (D, KV_HEADS * HEAD_DIM), D ** -0.5, 0.046875, ((0, 4), (1, 2)))
    w_value = scatter_about(seeds[4], (D, KV_HEADS * HEAD_DIM), D ** -0.5, 0.046875, ((0, 4), (1, 2)))
    w_out = scatter_about(seeds[5], (HEADS * HEAD_DIM, D), (HEADS * HEAD_DIM) ** -0.5, 0.0625, ((0, 2), (1, 4)))
    k_cache = draw_k_cache(jax.random.fold_in(seeds[14], 71), 0)
    v_cache = draw_v_cache(jax.random.fold_in(seeds[14], 71), 0)
    hist_lens = draw_hist_lens(jax.random.fold_in(seeds[14], 71), 0)
    parents = draw_parents(jax.random.fold_in(seeds[14], 71), 0)
    low_feats = draw_low_feats(jax.random.fold_in(seeds[14], 71), 0)
    mid_feats = draw_mid_feats(jax.random.fold_in(seeds[14], 71), 0)
    join_weight = draw_join_weight(jax.random.fold_in(seeds[14], 71), 0)
    draft_gain = jnp.clip(1.0 + 0.18 * jax.random.normal(seeds[13], (DRAFT_OUT,), jnp.float32), 0.099609375, 1.8984375).astype(jnp.bfloat16)
    return {"tree_states": tree_states, "attn_gain": attn_gain, "w_query": w_query, "w_key": w_key, "w_value": w_value, "w_out": w_out, "k_cache": k_cache, "v_cache": v_cache, "hist_lens": hist_lens, "parents": parents, "low_feats": low_feats, "mid_feats": mid_feats, "join_weight": join_weight, "draft_gain": draft_gain}


EPS = 1e-05
ROPE_BASE = 500000.0
MASKED = -1e+30

def rotate(vectors, places):
    halfway = vectors.shape[-1] // 2
    exponent = jnp.arange(halfway, dtype=jnp.float32) * (2.0 / vectors.shape[-1])
    frequency = jnp.power(ROPE_BASE, -exponent)
    angles = places.astype(jnp.float32)[..., None] * frequency
    cosine = jnp.cos(angles)
    sine_part = jnp.sin(angles)
    first_half = vectors[..., :halfway]
    second_half = vectors[..., halfway:]
    return jnp.concatenate([first_half * cosine - second_half * sine_part, second_half * cosine + first_half * sine_part], axis=-1)

def ancestry(parents):
    length = parents.shape[-1]
    indices = jnp.arange(length, dtype=jnp.int32)
    parent_link = (parents[..., :, None] == indices[None, :]).astype(jnp.float32)
    reached = jnp.minimum(parent_link + jnp.eye(length, dtype=jnp.float32), 1.0)
    for doubling in range(length.bit_length()):
        reached = jnp.minimum(jnp.einsum('cij,cjk->cik', reached, reached, precision=lax.Precision.HIGHEST), 1.0)
    return reached

def rounded(values):
    return lax.optimization_barrier(values.astype(jnp.bfloat16)).astype(jnp.float32)

def reference(tree_states, attn_gain, w_query, w_key, w_value, w_out, k_cache, v_cache, hist_lens, parents, low_feats, mid_feats, join_weight, draft_gain):
    states = tree_states.astype(jnp.float32)
    mean_square = lax.optimization_barrier(jnp.mean(states * states, axis=-1, keepdims=True))
    normed = (states * lax.rsqrt(mean_square + EPS) * attn_gain.astype(jnp.float32)).astype(jnp.bfloat16)
    flat_rows = normed.reshape(CONV * TREE, D)
    queries = jnp.dot(flat_rows, w_query, preferred_element_type=jnp.float32).reshape(CONV, TREE, HEADS, HEAD_DIM)
    new_keys = jnp.dot(flat_rows, w_key, preferred_element_type=jnp.float32).reshape(CONV, TREE, KV_HEADS, HEAD_DIM)
    new_values = jnp.dot(flat_rows, w_value, preferred_element_type=jnp.float32).reshape(CONV, TREE, KV_HEADS, HEAD_DIM)
    reached = ancestry(parents)
    depths = (lax.optimization_barrier(jnp.sum(reached, axis=-1)) - 1.0).astype(jnp.int32)
    places = hist_lens[:, None].astype(jnp.int32) + depths
    queries = rotate(queries, places[:, :, None]).astype(jnp.bfloat16)
    new_keys = rotate(new_keys, places[:, :, None]).astype(jnp.bfloat16)
    new_values = new_values.astype(jnp.bfloat16)
    group_size = HEADS // KV_HEADS
    query_heads = queries.reshape(CONV, TREE, KV_HEADS, group_size, HEAD_DIM).transpose(0, 2, 1, 3, 4)
    cache_keys = k_cache.reshape(CONV, HIST, KV_HEADS, HEAD_DIM).transpose(0, 2, 1, 3)
    cache_values = v_cache.reshape(CONV, HIST, KV_HEADS, HEAD_DIM).transpose(0, 2, 1, 3)
    tree_keys = new_keys.transpose(0, 2, 1, 3)
    tree_values = new_values.transpose(0, 2, 1, 3)
    positions = jnp.arange(HIST, dtype=jnp.int32)
    score_scale = HEAD_DIM ** (-0.5)

    def per_conversation(operands):
        conv_queries, conv_keys, conv_values, conv_tree_keys, conv_tree_values, conv_length, visible = operands

        def per_head(head_operands):
            query_block, head_keys, head_values, head_tree_keys, head_tree_values = head_operands
            query_wide = query_block.astype(jnp.float32)
            cache_scores = jnp.einsum('tgd,pd->tgp', query_wide, head_keys.astype(jnp.float32)) * score_scale
            tree_scores = jnp.einsum('tgd,jd->tgj', query_wide, head_tree_keys.astype(jnp.float32)) * score_scale
            cache_scores = jnp.where((positions < conv_length)[None, None, :], cache_scores, MASKED)
            tree_scores = jnp.where((visible > 0.5)[:, None, :], tree_scores, MASKED)
            largest = jnp.maximum(lax.optimization_barrier(jnp.max(cache_scores, axis=-1)), lax.optimization_barrier(jnp.max(tree_scores, axis=-1)))
            cache_weights = rounded(jnp.exp(cache_scores - largest[..., None]))
            tree_weights = rounded(jnp.exp(tree_scores - largest[..., None]))
            totals = lax.optimization_barrier(jnp.sum(cache_weights, axis=-1)) + lax.optimization_barrier(jnp.sum(tree_weights, axis=-1))
            mixed = jnp.einsum('tgp,pd->tgd', cache_weights, head_values.astype(jnp.float32))
            mixed = mixed + jnp.einsum('tgj,jd->tgd', tree_weights, head_tree_values.astype(jnp.float32))
            return (mixed / totals[..., None]).astype(jnp.bfloat16)
        return lax.map(per_head, (conv_queries, conv_keys, conv_values, conv_tree_keys, conv_tree_values))
    attended = lax.map(per_conversation, (query_heads, cache_keys, cache_values, tree_keys, tree_values, hist_lens.astype(jnp.int32), reached))
    attended_rows = attended.transpose(0, 2, 1, 3, 4).reshape(CONV * TREE, HEADS * HEAD_DIM)
    attn_branch = jnp.dot(attended_rows, w_out, preferred_element_type=jnp.float32).astype(jnp.bfloat16).reshape(CONV, TREE, D)
    high_feats = (states + attn_branch.astype(jnp.float32)).astype(jnp.bfloat16)
    joined_rows = jnp.dot(low_feats.reshape(CONV * TREE, D), join_weight[0], preferred_element_type=jnp.float32)
    joined_rows = joined_rows + jnp.dot(mid_feats.reshape(CONV * TREE, D), join_weight[1], preferred_element_type=jnp.float32)
    joined_rows = joined_rows + jnp.dot(high_feats.reshape(CONV * TREE, D), join_weight[2], preferred_element_type=jnp.float32)
    joined_energy = lax.optimization_barrier(jnp.mean(joined_rows * joined_rows, axis=-1, keepdims=True))
    draft_input = (joined_rows * lax.rsqrt(joined_energy + EPS) * draft_gain.astype(jnp.float32)).astype(jnp.bfloat16)
    return (attn_branch, draft_input.reshape(CONV, TREE, DRAFT_OUT))
```

```python
import functools
import math

import jax
import jax.numpy as jnp
from jax import lax
from jax.experimental import pallas as pl
from jax.experimental.pallas import tpu as pltpu
from jax.sharding import PartitionSpec as P

HEAD_DIM = 128
EPS = 1e-05
ROPE_BASE = 500000.0
MASKED = -1e30


def angles_of(places):
    halfway = HEAD_DIM // 2
    exponent = jnp.arange(halfway, dtype=jnp.float32) * (2.0 / HEAD_DIM)
    frequency = jnp.power(ROPE_BASE, -exponent)
    angles = places.astype(jnp.float32)[..., None] * frequency
    return jnp.cos(angles), jnp.sin(angles)


def rotate(vectors, cosine, sine):
    halfway = HEAD_DIM // 2
    first, second = vectors[..., :halfway], vectors[..., halfway:]
    cosine, sine = cosine[:, :, None], sine[:, :, None]
    return jnp.concatenate(
        [first * cosine - second * sine, second * cosine + first * sine], axis=-1
    )


def ancestry(parents):
    length = parents.shape[-1]
    indices = jnp.arange(length, dtype=jnp.int32)
    parent_link = (parents[..., :, None] == indices[None, :]).astype(jnp.float32)
    reached = jnp.minimum(parent_link + jnp.eye(length, dtype=jnp.float32), 1.0)
    for doubling in range(length.bit_length()):
        half = reached.astype(jnp.bfloat16)
        reached = jnp.minimum(
            jnp.einsum("cij,cjk->cik", half, half, preferred_element_type=jnp.float32), 1.0
        )
    return reached


def partner(index, step, count):
    if count & (count - 1) == 0:
        return index ^ step
    return (index + step) % count


def source(index, step, count):
    if count & (count - 1) == 0:
        return index ^ step
    return (index - step) % count


def hop(value, axis, step, count):
    return lax.ppermute(value, axis, [(i, partner(i, step, count)) for i in range(count)])


def exchange(pick, axis, count):
    me = lax.axis_index(axis)
    return [hop(pick(partner(me, step, count)), axis, step, count) for step in range(1, count)]


def gather_columns(block, axis, count):
    me = lax.axis_index(axis)
    width = block.shape[-1]
    whole = jnp.zeros(block.shape[:-1] + (width * count,), block.dtype)
    lead = (0,) * (block.ndim - 1)
    whole = lax.dynamic_update_slice(whole, block, lead + (me * width,))
    arrived = exchange(lambda d: block, axis, count)
    for step, other in enumerate(arrived, 1):
        whole = lax.dynamic_update_slice(
            whole, other, lead + (source(me, step, count) * width,)
        )
    return whole


def sum_over(value, axes, count):
    total = value
    for step in range(1, count):
        total = total + hop(value, axes, step, count)
    return total


def attend_kernel(
    group, pieces, live_ref, q_ref, k_ref, v_ref, tk_ref, tv_ref, vis_ref, o_ref, lse_ref, m_ref, acc_ref
):
    chunk_at = pl.program_id(2)
    tree_len = q_ref.shape[1]
    chunk = k_ref.shape[1]
    per = group // pieces
    rows = per * tree_len
    live = live_ref[pl.program_id(0)] - chunk_at * chunk
    nt = (((1,), (1,)), ((), ()))

    def queries(piece):
        return jnp.concatenate(
            [
                q_ref[0, :, g * HEAD_DIM : (g + 1) * HEAD_DIM]
                for g in range(piece * per, (piece + 1) * per)
            ],
            axis=0,
        )

    @pl.when(chunk_at == 0)
    def _():
        keys = tk_ref[0]
        values = jnp.concatenate([tv_ref[0], jnp.ones_like(tv_ref[0])], axis=1)
        seen = jnp.concatenate([vis_ref[0]] * per, axis=0) > 0.5
        for piece in range(pieces):
            at = slice(piece * rows, (piece + 1) * rows)
            scores = lax.dot_general(queries(piece), keys, nt, preferred_element_type=jnp.float32)
            scores = jnp.where(seen, scores, MASKED)
            top = jnp.max(scores, axis=1, keepdims=True)
            weights = jnp.exp2(scores - top).astype(jnp.bfloat16)
            m_ref[at] = top
            acc_ref[at] = jnp.dot(weights, values, preferred_element_type=jnp.float32)

    def step(masked):
        keys = k_ref[0]
        values = jnp.concatenate([v_ref[0], jnp.ones_like(v_ref[0])], axis=1)
        for piece in range(pieces):
            at = slice(piece * rows, (piece + 1) * rows)
            scores = lax.dot_general(queries(piece), keys, nt, preferred_element_type=jnp.float32)
            if masked:
                place = lax.broadcasted_iota(jnp.int32, scores.shape, 1)
                scores = jnp.where(place < live, scores, MASKED)
            before = m_ref[at]
            top = jnp.maximum(before, jnp.max(scores, axis=1, keepdims=True))
            weights = jnp.exp2(scores - top).astype(jnp.bfloat16)
            m_ref[at] = top
            acc_ref[at] = acc_ref[at] * jnp.exp2(before - top) + jnp.dot(
                weights, values, preferred_element_type=jnp.float32
            )

    @pl.when(live >= chunk)
    def _():
        step(False)

    @pl.when((live > 0) & (live < chunk))
    def _():
        step(True)

    @pl.when(chunk_at == pl.num_programs(2) - 1)
    def _():
        for g in range(group):
            at = slice(g * tree_len, (g + 1) * tree_len)
            total = acc_ref[at, HEAD_DIM:]
            o_ref[0, :, g * HEAD_DIM : (g + 1) * HEAD_DIM] = (
                acc_ref[at, :HEAD_DIM] / total
            ).astype(jnp.bfloat16)
            lse_ref[0, 0, at] = m_ref[at] + jnp.log2(total)


def attend(live, queries, keys, values, tree_keys, tree_values, visible):
    convos, tree_len, width = queries.shape
    span = keys.shape[1]
    kv_here = keys.shape[2] // HEAD_DIM
    group = width // HEAD_DIM // kv_here
    share = tree_keys.shape[1]
    chunk = math.gcd(span, 1024)
    pieces = math.gcd(group, 4)
    rows = group * tree_len
    grid_spec = pltpu.PrefetchScalarGridSpec(
        num_scalar_prefetch=1,
        grid=(convos, kv_here, span // chunk),
        in_specs=[
            pl.BlockSpec((1, tree_len, group * HEAD_DIM), lambda c, h, p, s: (c, 0, h)),
            pl.BlockSpec((1, chunk, HEAD_DIM), lambda c, h, p, s: (c, p, h)),
            pl.BlockSpec((1, chunk, HEAD_DIM), lambda c, h, p, s: (c, p, h)),
            pl.BlockSpec((1, share, HEAD_DIM), lambda c, h, p, s: (c, 0, h)),
            pl.BlockSpec((1, share, HEAD_DIM), lambda c, h, p, s: (c, 0, h)),
            pl.BlockSpec((1, tree_len, share), lambda c, h, p, s: (c, 0, 0)),
        ],
        out_specs=[
            pl.BlockSpec((1, tree_len, group * HEAD_DIM), lambda c, h, p, s: (c, 0, h)),
            pl.BlockSpec((1, 1, rows, HEAD_DIM), lambda c, h, p, s: (c, h, 0, 0)),
        ],
        scratch_shapes=[
            pltpu.VMEM((rows, 1), jnp.float32),
            pltpu.VMEM((rows, 2 * HEAD_DIM), jnp.float32),
        ],
    )
    work = convos * kv_here * rows * span
    mixed, lse = pl.pallas_call(
        functools.partial(attend_kernel, group, pieces),
        grid_spec=grid_spec,
        out_shape=[
            jax.ShapeDtypeStruct((convos, tree_len, width), jnp.bfloat16),
            jax.ShapeDtypeStruct((convos, kv_here, rows, HEAD_DIM), jnp.float32),
        ],
        compiler_params=pltpu.CompilerParams(vmem_limit_bytes=40 * 1024 * 1024),
        cost_estimate=pl.CostEstimate(
            flops=6 * work * HEAD_DIM, bytes_accessed=20_000_000, transcendentals=work
        ),
        name="attend",
    )(live, queries, keys, values, tree_keys, tree_values, visible)
    lse = lse[..., 0].reshape(convos, kv_here * group, tree_len)
    return mixed, lse


def shards(
    width_all,
    draft_all,
    tree_states,
    attn_gain,
    w_query,
    w_key,
    w_value,
    w_out,
    k_cache,
    v_cache,
    hist_lens,
    parents,
    low_feats,
    mid_feats,
    join_weight,
    draft_gain,
):
    convos, tree_len, width_part = tree_states.shape
    rows = convos * tree_len
    n_seq, n_grp, n_mdl = (lax.axis_size(a) for a in ("seq", "grp", "mdl"))
    seq_at, grp_at, mdl_at = (lax.axis_index(a) for a in ("seq", "grp", "mdl"))
    heads_here = w_query.shape[1] // HEAD_DIM
    kv_here = w_key.shape[1] // HEAD_DIM
    tree_share = tree_len // n_seq
    head_share = heads_here // n_seq
    part = rows // n_mdl

    def own_rows(full, axis=0):
        return lax.dynamic_slice_in_dim(full, mdl_at * part, part, axis)

    def ring(own):
        held, blocks = own, []
        for _ in range(1, n_grp):
            held = lax.ppermute(held, "grp", [(i, (i + 1) % n_grp) for i in range(n_grp)])
            blocks.append(held)
        return blocks

    def both(block, axis=0):
        return jnp.concatenate([block] + exchange(lambda d: block, "mdl", n_mdl), axis=axis)

    def own_first(full):
        pieces = full.reshape((n_mdl, part) + full.shape[1:])
        order = [source(mdl_at, step, n_mdl) for step in range(n_mdl)]
        return jnp.concatenate(
            [lax.dynamic_index_in_dim(pieces, at, 0, keepdims=False) for at in order], axis=0
        )

    low_rows = low_feats.reshape(rows, width_part)
    mid_rows = mid_feats.reshape(rows, width_part)
    early = jnp.stack([own_rows(low_rows), own_rows(mid_rows)])
    early_blocks = ring(early)

    states = tree_states.astype(jnp.float32)
    energy = sum_over(jnp.sum(states * states, axis=-1), "seq", n_seq)
    row_scale = lax.rsqrt(energy / width_all + EPS)
    flat_rows = (states * attn_gain.astype(jnp.float32)).astype(jnp.bfloat16)
    flat_rows = flat_rows.reshape(rows, width_part)
    key_part = jnp.dot(flat_rows, w_key, preferred_element_type=jnp.float32)
    value_part = jnp.dot(flat_rows, w_value, preferred_element_type=jnp.float32)
    query_part = jnp.dot(flat_rows, w_query, preferred_element_type=jnp.float32)
    reached = ancestry(parents)
    depths = (jnp.sum(reached, axis=-1) - 1.0).astype(jnp.int32)
    cosine, sine = angles_of(hist_lens[:, None] + depths)

    def share(full, at=seq_at, axis=1):
        return lax.dynamic_slice_in_dim(full, at * tree_share, tree_share, axis)

    both_part = jnp.concatenate([key_part, value_part], axis=1).reshape(convos, tree_len, -1)
    new = share(both_part)
    wide = both_part.astype(jnp.bfloat16)
    for other in exchange(lambda d: share(wide, d), "seq", n_seq):
        new = new + other.astype(jnp.float32)
    new = new * share(row_scale)[..., None]
    new = new.reshape(convos, tree_share, 2 * kv_here, HEAD_DIM)
    tree_keys = rotate(new[:, :, :kv_here], share(cosine), share(sine)).astype(jnp.bfloat16)
    tree_values = new[:, :, kv_here:].astype(jnp.bfloat16)
    tree_keys = tree_keys.reshape(convos, tree_share, -1)
    tree_values = tree_values.reshape(convos, tree_share, -1)

    head_width = head_share * HEAD_DIM

    def columns(full, at):
        return lax.dynamic_slice_in_dim(full, at * head_width, head_width, full.ndim - 1)

    summed = columns(query_part, seq_at)
    sent = query_part.astype(jnp.bfloat16)
    for other in exchange(lambda d: columns(sent, d), "seq", n_seq):
        summed = summed + other.astype(jnp.float32)
    factor = row_scale * (HEAD_DIM**-0.5 * math.log2(math.e))
    summed = summed.reshape(convos, tree_len, head_share, HEAD_DIM) * factor[:, :, None, None]
    queries = rotate(summed, cosine, sine).astype(jnp.bfloat16)
    queries = gather_columns(queries.reshape(convos, tree_len, head_width), "seq", n_seq)

    span = k_cache.shape[1]
    live = jnp.clip(hist_lens - seq_at * span, 0, span)
    mixed, lse = attend(
        live, queries, k_cache, v_cache, tree_keys, tree_values, share(reached, axis=2)
    )

    def lse_share(at):
        return lax.dynamic_slice_in_dim(lse, at * head_share, head_share, 1)

    logs = [lse_share(seq_at)] + exchange(lse_share, "seq", n_seq)
    parts = [columns(mixed, seq_at)] + exchange(lambda d: columns(mixed, d), "seq", n_seq)
    top = functools.reduce(jnp.maximum, logs)
    weights = [jnp.exp2(log - top) for log in logs]
    total = sum(weights)
    attended = 0.0
    for weight, values in zip(weights, parts):
        weight = (weight / total).transpose(0, 2, 1)[..., None]
        attended = attended + weight * values.astype(jnp.float32).reshape(
            convos, tree_len, head_share, HEAD_DIM
        )
    attended = attended.astype(jnp.bfloat16).reshape(rows, head_width)
    attended = gather_columns(attended, "seq", n_seq)
    branch = jnp.dot(attended, w_out, preferred_element_type=jnp.float32)
    branch_own = own_rows(branch)
    for other in exchange(
        lambda d: lax.dynamic_slice_in_dim(branch, d * part, part, 0), "mdl", n_mdl
    ):
        branch_own = branch_own + other
    branch_own = branch_own.astype(jnp.bfloat16)
    state_rows = tree_states.reshape(rows, width_part)
    high_own = (
        own_rows(state_rows).astype(jnp.float32) + branch_own.astype(jnp.float32)
    ).astype(jnp.bfloat16)
    high_blocks = ring(high_own)

    pieces = [branch_own] + exchange(lambda d: branch_own, "mdl", n_mdl)
    attn_branch = jnp.zeros((rows, width_part), jnp.bfloat16)
    for step, piece in enumerate(pieces):
        attn_branch = lax.dynamic_update_slice(
            attn_branch, piece, (source(mdl_at, step, n_mdl) * part, 0)
        )
    high_here = jnp.concatenate(pieces, axis=0).astype(jnp.float32)
    high_here = (own_first(state_rows).astype(jnp.float32) + high_here).astype(jnp.bfloat16)

    out_part = join_weight.shape[2]

    def dot(a, b):
        return jnp.dot(a, b, preferred_element_type=jnp.float32)

    joined = jnp.zeros((n_grp * convos, tree_share, out_part), jnp.float32)
    convo_part = convos // n_mdl
    for step in range(n_grp):
        if step == 0:
            low, mid, high = own_first(low_rows), own_first(mid_rows), high_here
        else:
            pair = both(early_blocks[step - 1], axis=1)
            low, mid, high = pair[0], pair[1], both(high_blocks[step - 1])
        first = dot(low, join_weight[0]) + dot(mid, join_weight[1])
        block = first + dot(high, join_weight[2])
        block = block.reshape(convos, tree_len, out_part)
        mine = share(block)
        block = block.astype(jnp.bfloat16)
        for other in exchange(lambda d: share(block, d), "seq", n_seq):
            mine = mine + other.astype(jnp.float32)
        origin = (grp_at + n_grp - step) % n_grp
        for turn in range(n_mdl):
            at = origin * convos + source(mdl_at, turn, n_mdl) * convo_part
            joined = lax.dynamic_update_slice(
                joined, mine[turn * convo_part : (turn + 1) * convo_part], (at, 0, 0)
            )
    joined_energy = sum_over(
        jnp.sum(joined * joined, axis=-1), ("grp", "mdl"), n_grp * n_mdl
    )
    draft_input = (
        joined
        * lax.rsqrt(joined_energy / draft_all + EPS)[..., None]
        * draft_gain.astype(jnp.float32)
    ).astype(jnp.bfloat16)
    return (attn_branch.reshape(convos, tree_len, width_part), draft_input)


def solution(mesh):
    in_specs = (
        P("grp", None, "seq"),
        P("seq"),
        P("seq", "mdl"),
        P("seq", "mdl"),
        P("seq", "mdl"),
        P("mdl", "seq"),
        P("grp", "seq", "mdl"),
        P("grp", "seq", "mdl"),
        P("grp"),
        P("grp", None),
        P("grp", None, "seq"),
        P("grp", None, "seq"),
        P(None, "seq", ("grp", "mdl")),
        P(("grp", "mdl")),
    )
    out_specs = (P("grp", None, "seq"), P(None, "seq", ("grp", "mdl")))

    def run(*args):
        body = functools.partial(shards, args[0].shape[-1], args[-1].shape[0])
        return jax.shard_map(
            body, mesh=mesh, in_specs=in_specs, out_specs=out_specs, check_vma=False
        )(*args)

    return run
```

```python
import functools
import math

import jax
import jax.numpy as jnp
from jax import lax
from jax.experimental import pallas as pl
from jax.experimental.pallas import tpu as pltpu
from jax.sharding import PartitionSpec as P

HEAD_DIM = 128
EPS = 1e-05
ROPE_BASE = 500000.0
MASKED = -1e30


def angles_of(places):
    halfway = HEAD_DIM // 2
    exponent = jnp.arange(halfway, dtype=jnp.float32) * (2.0 / HEAD_DIM)
    frequency = jnp.power(ROPE_BASE, -exponent)
    angles = places.astype(jnp.float32)[..., None] * frequency
    return jnp.cos(angles), jnp.sin(angles)


def rotate(vectors, cosine, sine):
    halfway = HEAD_DIM // 2
    first, second = vectors[..., :halfway], vectors[..., halfway:]
    cosine, sine = cosine[:, :, None], sine[:, :, None]
    return jnp.concatenate(
        [first * cosine - second * sine, second * cosine + first * sine], axis=-1
    )


def ancestry(parents):
    length = parents.shape[-1]
    indices = jnp.arange(length, dtype=jnp.int32)
    parent_link = (parents[..., :, None] == indices[None, :]).astype(jnp.float32)
    reached = jnp.minimum(parent_link + jnp.eye(length, dtype=jnp.float32), 1.0)
    for doubling in range(length.bit_length()):
        half = reached.astype(jnp.bfloat16)
        reached = jnp.minimum(
            jnp.einsum("cij,cjk->cik", half, half, preferred_element_type=jnp.float32), 1.0
        )
    return reached


def partner(index, step, count):
    if count & (count - 1) == 0:
        return index ^ step
    return (index + step) % count


def source(index, step, count):
    if count & (count - 1) == 0:
        return index ^ step
    return (index - step) % count


def hop(value, axis, step, count):
    return lax.ppermute(value, axis, [(i, partner(i, step, count)) for i in range(count)])


def exchange(pick, axis, count):
    me = lax.axis_index(axis)
    return [hop(pick(partner(me, step, count)), axis, step, count) for step in range(1, count)]


def gather_columns(block, axis, count):
    me = lax.axis_index(axis)
    width = block.shape[-1]
    whole = jnp.zeros(block.shape[:-1] + (width * count,), block.dtype)
    lead = (0,) * (block.ndim - 1)
    whole = lax.dynamic_update_slice(whole, block, lead + (me * width,))
    arrived = exchange(lambda d: block, axis, count)
    for step, other in enumerate(arrived, 1):
        whole = lax.dynamic_update_slice(
            whole, other, lead + (source(me, step, count) * width,)
        )
    return whole


def sum_over(value, axes, count):
    total = value
    for step in range(1, count):
        total = total + hop(value, axes, step, count)
    return total


def attend_kernel(
    group, pieces, live_ref, q_ref, k_ref, v_ref, tk_ref, tv_ref, vis_ref, o_ref, lse_ref, m_ref, acc_ref
):
    chunk_at = pl.program_id(2)
    tree_len = q_ref.shape[1]
    chunk = k_ref.shape[1]
    per = group // pieces
    rows = per * tree_len
    live = live_ref[pl.program_id(0)] - chunk_at * chunk
    nt = (((1,), (1,)), ((), ()))

    def queries(piece):
        return jnp.concatenate(
            [
                q_ref[0, :, g * HEAD_DIM : (g + 1) * HEAD_DIM]
                for g in range(piece * per, (piece + 1) * per)
            ],
            axis=0,
        )

    @pl.when(chunk_at == 0)
    def _():
        keys = tk_ref[0]
        values = jnp.concatenate([tv_ref[0], jnp.ones_like(tv_ref[0])], axis=1)
        seen = jnp.concatenate([vis_ref[0]] * per, axis=0) > 0.5
        for piece in range(pieces):
            at = slice(piece * rows, (piece + 1) * rows)
            scores = lax.dot_general(queries(piece), keys, nt, preferred_element_type=jnp.float32)
            scores = jnp.where(seen, scores, MASKED)
            top = jnp.max(scores, axis=1, keepdims=True)
            weights = jnp.exp2(scores - top).astype(jnp.bfloat16)
            m_ref[at] = top
            acc_ref[at] = jnp.dot(weights, values, preferred_element_type=jnp.float32)

    def step(masked):
        keys = k_ref[0]
        values = jnp.concatenate([v_ref[0], jnp.ones_like(v_ref[0])], axis=1)
        for piece in range(pieces):
            at = slice(piece * rows, (piece + 1) * rows)
            scores = lax.dot_general(queries(piece), keys, nt, preferred_element_type=jnp.float32)
            if masked:
                place = lax.broadcasted_iota(jnp.int32, scores.shape, 1)
                scores = jnp.where(place < live, scores, MASKED)
            before = m_ref[at]
            top = jnp.maximum(before, jnp.max(scores, axis=1, keepdims=True))
            weights = jnp.exp2(scores - top).astype(jnp.bfloat16)
            m_ref[at] = top
            acc_ref[at] = acc_ref[at] * jnp.exp2(before - top) + jnp.dot(
                weights, values, preferred_element_type=jnp.float32
            )

    @pl.when(live >= chunk)
    def _():
        step(False)

    @pl.when((live > 0) & (live < chunk))
    def _():
        step(True)

    @pl.when(chunk_at == pl.num_programs(2) - 1)
    def _():
        for g in range(group):
            at = slice(g * tree_len, (g + 1) * tree_len)
            total = acc_ref[at, HEAD_DIM:]
            o_ref[0, :, g * HEAD_DIM : (g + 1) * HEAD_DIM] = (
                acc_ref[at, :HEAD_DIM] / total
            ).astype(jnp.bfloat16)
            lse_ref[0, 0, at] = m_ref[at] + jnp.log2(total)


def attend(live, queries, keys, values, tree_keys, tree_values, visible):
    convos, tree_len, width = queries.shape
    span = keys.shape[1]
    kv_here = keys.shape[2] // HEAD_DIM
    group = width // HEAD_DIM // kv_here
    share = tree_keys.shape[1]
    chunk = math.gcd(span, 1024)
    pieces = math.gcd(group, 4)
    rows = group * tree_len
    grid_spec = pltpu.PrefetchScalarGridSpec(
        num_scalar_prefetch=1,
        grid=(convos, kv_here, span // chunk),
        in_specs=[
            pl.BlockSpec((1, tree_len, group * HEAD_DIM), lambda c, h, p, s: (c, 0, h)),
            pl.BlockSpec((1, chunk, HEAD_DIM), lambda c, h, p, s: (c, p, h)),
            pl.BlockSpec((1, chunk, HEAD_DIM), lambda c, h, p, s: (c, p, h)),
            pl.BlockSpec((1, share, HEAD_DIM), lambda c, h, p, s: (c, 0, h)),
            pl.BlockSpec((1, share, HEAD_DIM), lambda c, h, p, s: (c, 0, h)),
            pl.BlockSpec((1, tree_len, share), lambda c, h, p, s: (c, 0, 0)),
        ],
        out_specs=[
            pl.BlockSpec((1, tree_len, group * HEAD_DIM), lambda c, h, p, s: (c, 0, h)),
            pl.BlockSpec((1, 1, rows, HEAD_DIM), lambda c, h, p, s: (c, h, 0, 0)),
        ],
        scratch_shapes=[
            pltpu.VMEM((rows, 1), jnp.float32),
            pltpu.VMEM((rows, 2 * HEAD_DIM), jnp.float32),
        ],
    )
    work = convos * kv_here * rows * span
    mixed, lse = pl.pallas_call(
        functools.partial(attend_kernel, group, pieces),
        grid_spec=grid_spec,
        out_shape=[
            jax.ShapeDtypeStruct((convos, tree_len, width), jnp.bfloat16),
            jax.ShapeDtypeStruct((convos, kv_here, rows, HEAD_DIM), jnp.float32),
        ],
        compiler_params=pltpu.CompilerParams(vmem_limit_bytes=40 * 1024 * 1024),
        cost_estimate=pl.CostEstimate(
            flops=6 * work * HEAD_DIM, bytes_accessed=20_000_000, transcendentals=work
        ),
        name="attend",
    )(live, queries, keys, values, tree_keys, tree_values, visible)
    lse = lse[..., 0].reshape(convos, kv_here * group, tree_len)
    return mixed, lse


def shards(
    width_all,
    draft_all,
    tree_states,
    attn_gain,
    w_query,
    w_key,
    w_value,
    w_out,
    k_cache,
    v_cache,
    hist_lens,
    parents,
    low_feats,
    mid_feats,
    join_weight,
    draft_gain,
):
    convos, tree_len, width_part = tree_states.shape
    rows = convos * tree_len
    n_seq, n_grp, n_mdl = (lax.axis_size(a) for a in ("seq", "grp", "mdl"))
    seq_at, grp_at, mdl_at = (lax.axis_index(a) for a in ("seq", "grp", "mdl"))
    heads_here = w_query.shape[1] // HEAD_DIM
    kv_here = w_key.shape[1] // HEAD_DIM
    tree_share = tree_len // n_seq
    head_share = heads_here // n_seq
    part = rows // n_mdl

    def own_rows(full, axis=0):
        return lax.dynamic_slice_in_dim(full, mdl_at * part, part, axis)

    def ring(own):
        held, blocks = own, []
        for _ in range(1, n_grp):
            held = lax.ppermute(held, "grp", [(i, (i + 1) % n_grp) for i in range(n_grp)])
            blocks.append(held)
        return blocks

    def both(block, axis=0):
        return jnp.concatenate([block] + exchange(lambda d: block, "mdl", n_mdl), axis=axis)

    def own_first(full):
        pieces = full.reshape((n_mdl, part) + full.shape[1:])
        order = [source(mdl_at, step, n_mdl) for step in range(n_mdl)]
        return jnp.concatenate(
            [lax.dynamic_index_in_dim(pieces, at, 0, keepdims=False) for at in order], axis=0
        )

    low_rows = low_feats.reshape(rows, width_part)
    mid_rows = mid_feats.reshape(rows, width_part)
    early = jnp.stack([own_rows(low_rows), own_rows(mid_rows)])
    early_blocks = []

    def advance(value):
        if len(early_blocks) < n_grp - 1:
            held = early_blocks[-1] if early_blocks else early
            held = lax.ppermute(held, "grp", [(i, (i + 1) % n_grp) for i in range(n_grp)])
            value, held = lax.optimization_barrier((value, held))
            early_blocks.append(held)
        return value

    states = tree_states.astype(jnp.float32)
    energy = sum_over(jnp.sum(states * states, axis=-1), "seq", n_seq)
    row_scale = lax.rsqrt(energy / width_all + EPS)
    flat_rows = (states * attn_gain.astype(jnp.float32)).astype(jnp.bfloat16)
    flat_rows = flat_rows.reshape(rows, width_part)
    key_part = jnp.dot(flat_rows, w_key, preferred_element_type=jnp.float32)
    value_part = jnp.dot(flat_rows, w_value, preferred_element_type=jnp.float32)
    query_part = jnp.dot(flat_rows, w_query, preferred_element_type=jnp.float32)
    reached = ancestry(parents)
    depths = (jnp.sum(reached, axis=-1) - 1.0).astype(jnp.int32)
    cosine, sine = angles_of(hist_lens[:, None] + depths)

    def share(full, at=seq_at, axis=1):
        return lax.dynamic_slice_in_dim(full, at * tree_share, tree_share, axis)

    both_part = jnp.concatenate([key_part, value_part], axis=1).reshape(convos, tree_len, -1)
    new = share(both_part)
    wide = both_part.astype(jnp.bfloat16)
    for other in exchange(lambda d: share(wide, d), "seq", n_seq):
        new = new + other.astype(jnp.float32)
    new = new * share(row_scale)[..., None]
    new = new.reshape(convos, tree_share, 2 * kv_here, HEAD_DIM)
    tree_keys = rotate(new[:, :, :kv_here], share(cosine), share(sine)).astype(jnp.bfloat16)
    tree_values = new[:, :, kv_here:].astype(jnp.bfloat16)
    tree_keys = tree_keys.reshape(convos, tree_share, -1)
    tree_values = tree_values.reshape(convos, tree_share, -1)

    head_width = head_share * HEAD_DIM

    def columns(full, at):
        return lax.dynamic_slice_in_dim(full, at * head_width, head_width, full.ndim - 1)

    summed = columns(query_part, seq_at)
    sent = query_part.astype(jnp.bfloat16)
    for other in exchange(lambda d: columns(sent, d), "seq", n_seq):
        summed = summed + other.astype(jnp.float32)
    factor = row_scale * (HEAD_DIM**-0.5 * math.log2(math.e))
    summed = summed.reshape(convos, tree_len, head_share, HEAD_DIM) * factor[:, :, None, None]
    queries = rotate(summed, cosine, sine).astype(jnp.bfloat16)
    queries = advance(queries.reshape(convos, tree_len, head_width))
    queries = gather_columns(queries, "seq", n_seq)

    span = k_cache.shape[1]
    live = jnp.clip(hist_lens - seq_at * span, 0, span)
    mixed, lse = attend(
        live, queries, k_cache, v_cache, tree_keys, tree_values, share(reached, axis=2)
    )

    mixed = advance(mixed)

    def lse_share(at):
        return lax.dynamic_slice_in_dim(lse, at * head_share, head_share, 1)

    logs = [lse_share(seq_at)] + exchange(lse_share, "seq", n_seq)
    parts = [columns(mixed, seq_at)] + exchange(lambda d: columns(mixed, d), "seq", n_seq)
    top = functools.reduce(jnp.maximum, logs)
    weights = [jnp.exp2(log - top) for log in logs]
    total = sum(weights)
    attended = 0.0
    for weight, values in zip(weights, parts):
        weight = (weight / total).transpose(0, 2, 1)[..., None]
        attended = attended + weight * values.astype(jnp.float32).reshape(
            convos, tree_len, head_share, HEAD_DIM
        )
    attended = attended.astype(jnp.bfloat16).reshape(rows, head_width)
    attended = gather_columns(attended, "seq", n_seq)
    attended = advance(attended)
    while len(early_blocks) < n_grp - 1:
        attended = advance(attended)
    branch = jnp.dot(attended, w_out, preferred_element_type=jnp.float32)
    branch_own = own_rows(branch)
    for other in exchange(
        lambda d: lax.dynamic_slice_in_dim(branch, d * part, part, 0), "mdl", n_mdl
    ):
        branch_own = branch_own + other
    branch_own = branch_own.astype(jnp.bfloat16)
    state_rows = tree_states.reshape(rows, width_part)
    high_own = (
        own_rows(state_rows).astype(jnp.float32) + branch_own.astype(jnp.float32)
    ).astype(jnp.bfloat16)
    high_blocks = ring(high_own)

    pieces = [branch_own] + exchange(lambda d: branch_own, "mdl", n_mdl)
    attn_branch = jnp.zeros((rows, width_part), jnp.bfloat16)
    for step, piece in enumerate(pieces):
        attn_branch = lax.dynamic_update_slice(
            attn_branch, piece, (source(mdl_at, step, n_mdl) * part, 0)
        )
    high_here = jnp.concatenate(pieces, axis=0).astype(jnp.float32)
    high_here = (own_first(state_rows).astype(jnp.float32) + high_here).astype(jnp.bfloat16)

    out_part = join_weight.shape[2]

    def dot(a, b):
        return jnp.dot(a, b, preferred_element_type=jnp.float32)

    joined = jnp.zeros((n_grp * convos, tree_share, out_part), jnp.float32)
    convo_part = convos // n_mdl
    for step in range(n_grp):
        if step == 0:
            low, mid, high = own_first(low_rows), own_first(mid_rows), high_here
        else:
            pair = both(early_blocks[step - 1], axis=1)
            low, mid, high = pair[0], pair[1], both(high_blocks[step - 1])
        first = dot(low, join_weight[0]) + dot(mid, join_weight[1])
        block = first + dot(high, join_weight[2])
        block = block.reshape(convos, tree_len, out_part)
        mine = share(block)
        block = block.astype(jnp.bfloat16)
        for other in exchange(lambda d: share(block, d), "seq", n_seq):
            mine = mine + other.astype(jnp.float32)
        origin = (grp_at + n_grp - step) % n_grp
        for turn in range(n_mdl):
            at = origin * convos + source(mdl_at, turn, n_mdl) * convo_part
            joined = lax.dynamic_update_slice(
                joined, mine[turn * convo_part : (turn + 1) * convo_part], (at, 0, 0)
            )
    joined_energy = sum_over(
        jnp.sum(joined * joined, axis=-1), ("grp", "mdl"), n_grp * n_mdl
    )
    draft_input = (
        joined
        * lax.rsqrt(joined_energy / draft_all + EPS)[..., None]
        * draft_gain.astype(jnp.float32)
    ).astype(jnp.bfloat16)
    return (attn_branch.reshape(convos, tree_len, width_part), draft_input)


def solution(mesh):
    in_specs = (
        P("grp", None, "seq"),
        P("seq"),
        P("seq", "mdl"),
        P("seq", "mdl"),
        P("seq", "mdl"),
        P("mdl", "seq"),
        P("grp", "seq", "mdl"),
        P("grp", "seq", "mdl"),
        P("grp"),
        P("grp", None),
        P("grp", None, "seq"),
        P("grp", None, "seq"),
        P(None, "seq", ("grp", "mdl")),
        P(("grp", "mdl")),
    )
    out_specs = (P("grp", None, "seq"), P(None, "seq", ("grp", "mdl")))

    def run(*args):
        body = functools.partial(shards, args[0].shape[-1], args[-1].shape[0])
        return jax.shard_map(
            body, mesh=mesh, in_specs=in_specs, out_specs=out_specs, check_vma=False
        )(*args)

    return run
```
